32 devices in a mesh: energy: 32 (over z, y, x, core), slab: 1.
Axes of the slice: x: 2, y: 2, z: 4, core: 2. Of those that a mesh axis runs over, the one named last changes fastest.
Arguments:
- green_less: bfloat16 [2, 128, 32, 2592], P('slab', 'energy'), may hold values from -6 to 6
- coupling: bfloat16 [2, 32, 64, 1296], P(None, 'energy', 'slab'), may hold values from -0.375 to 0.375
- occupation: float32 [64], replicated, may hold values from 0.1 to 3
- shift_index: int32 [64], replicated, may hold values from 1 to 64, as said below
Outputs:
- sigma_less: bfloat16 [2, 128, 32, 2592], P('slab', 'energy')
The draws below stay inside these ranges and needn't reach their ends.
Inputs may be any that keep to these rules, and one draw needn't show every extreme that they name: `shift_index`: every value of 1 to 64 may occur; 1 and 64 occur in every draw.
All inputs are finite; a program needn't handle non-finite values.
Results may differ from the reference program's by a relative error of at most 0.0057.
Values may be sent and summed in bfloat16 or wider, within the bound.
A program may use at most 128 MiB of HBM per device.

```python
import math
import jax
import jax.numpy as jnp
from jax import lax

O = 36
MODES = 64
NE = 128
ELEMS = 32
SHIFTS = 64


def draw_shift_index(key, part):
    values = jax.random.randint(key, (MODES,), 1, SHIFTS + 1)
    spot = jax.random.randint(jax.random.fold_in(key, 7), (), 0, MODES)
    offset = jax.random.randint(jax.random.fold_in(key, 11), (), 1, MODES)
    values = values.at[spot].set(SHIFTS)
    values = values.at[(spot + offset) % MODES].set(1)
    return values.astype(jnp.int32)


def level_of(key, dims, shards, low, high):
    def one(position, shards_of):
        draws = jax.random.uniform(jax.random.fold_in(jax.random.fold_in(key, 6), position), (shards_of,), jnp.float32, low / len(shards), high / len(shards))
        return jnp.repeat(jnp.exp(draws), dims[position] // shards_of).reshape((-1,) + (1,) * (len(dims) - position - 1))

    loudness = one(*shards[0])
    for cut in shards[1:]:
        loudness = loudness * one(*cut)
    return loudness


def scatter_about(own_key, dims, deviation, most, shards=(), kind=jnp.bfloat16):
    factor_of = level_of(own_key, dims, shards, -0.22, 0.18) if shards else 1.0
    values = jax.random.normal(own_key, dims, jnp.float32) * deviation * factor_of
    return jnp.minimum(jnp.maximum(values, -most), most).astype(kind)


def setup_inputs(seed: int = 0) -> dict:
    key_list = jax.random.split(jax.random.key(seed), 5)
    return {
        "green_less": scatter_about(key_list[0], (2, NE, ELEMS, 2 * O * O), 1.0, 6.0, ((1, 32),)),
        "coupling": scatter_about(key_list[1], (2, ELEMS, MODES, O * O), (O * MODES // 8) ** -0.5, 0.375, ((1, 32),)),
        "occupation": jnp.clip(jnp.exp(jax.random.uniform(key_list[2], (MODES,), jnp.float32, math.log(0.1), math.log(3.0))), 0.1, 3.0),
        "shift_index": draw_shift_index(jax.random.fold_in(key_list[4], 71), 0),
    }


def correlate(green, mats_flat, occ, shifts):
    count_e, count_b, flat = green.shape
    orbs = math.isqrt(flat // 2)
    span = count_e // 2
    modes = mats_flat.shape[1]
    group = math.gcd(16, modes)
    blocks = green.reshape(count_e, count_b, 2, orbs, orbs)
    padded = jnp.pad(blocks, ((span, span), (0, 0), (0, 0), (0, 0), (0, 0)))
    mats = mats_flat.reshape(count_b, modes // group, group, orbs, orbs).transpose(1, 0, 2, 3, 4)
    occ_groups = occ.reshape(modes // group, group)
    shift_groups = shifts.reshape(modes // group, group)

    def pick(amount):
        upper = lax.dynamic_slice_in_dim(padded, (span + amount).astype(jnp.int32), count_e, 0)
        lower = lax.dynamic_slice_in_dim(padded, (span - amount).astype(jnp.int32), count_e, 0)
        return (upper, lower)

    def advance(total, item):
        mat, weight, amount = item
        upper, lower = jax.vmap(pick)(amount)
        scale = weight[:, None, None, None, None, None]
        shifted = ((scale + 1.0) * upper.astype(jnp.float32) + scale * lower.astype(jnp.float32)).astype(jnp.bfloat16)
        left = jnp.einsum('bmai,mebpij->mebpaj', mat.astype(jnp.float32), shifted.astype(jnp.float32)).astype(jnp.bfloat16)
        total = total + jnp.einsum('mebpaj,bmcj->ebpac', left.astype(jnp.float32), mat.astype(jnp.float32))
        return (total, None)
    start = jnp.zeros((count_e, count_b, 2, orbs, orbs), jnp.float32)
    total, _ = lax.scan(advance, start, (mats, occ_groups, shift_groups))
    return total.reshape(count_e, count_b, flat)

def reference(green_less, coupling, occupation, shift_index):
    slabs, count_e, count_b, flat = green_less.shape
    items = green_less.transpose(0, 2, 1, 3).reshape(slabs * count_b, count_e, 1, flat)
    mats = coupling.reshape(slabs * count_b, 1, coupling.shape[2], coupling.shape[3])

    def one_block(pair):
        green, mat = pair
        return correlate(green, mat, occupation, shift_index).astype(jnp.bfloat16)
    result = lax.map(one_block, (items, mats))
    return result.reshape(slabs, count_b, count_e, flat).transpose(0, 2, 1, 3)
```

```python
import functools
import math

import jax
import jax.numpy as jnp
from jax import lax
from jax.experimental import pallas as pl
from jax.experimental.pallas import tpu as pltpu
from jax.sharding import PartitionSpec as P

LANES = 256


def partner_2(value, axis, distance):
    mask = 2**distance
    pairs = [(source, source ^ mask) for source in range(lax.axis_size(axis))]
    return lax.ppermute(value, axis, pairs)


def ceil_div(a, b):
    return (a + b - 1) // b


def kernel(
    sizes, occ_ref, shift_ref, green_ref, coup_ref, pair_ref, out_ref, copies, diag, rights, acc
):
    orbs, per, tiles, pad_tiles, stored, group, rows, slot = sizes
    used = per * orbs
    modes = coup_ref.shape[0]
    pad = pad_tiles * per

    copies[...] = jnp.zeros_like(copies)
    lane = lax.broadcasted_iota(jnp.int32, (rows, LANES), 1)

    @pl.loop(0, tiles + 1)
    def _(t):
        here = green_ref[t].astype(jnp.float32)
        after = green_ref[t + 1].astype(jnp.float32)
        at = pad_tiles - 1 + t
        copies[0, at] = here
        for r in range(1, per):
            cut = used - orbs * r
            copies[r, at] = jnp.where(
                lane < cut,
                pltpu.roll(here, LANES - orbs * r, 1),
                pltpu.roll(after, cut, 1),
            )

    rights[...] = jnp.zeros_like(rights)
    acc[...] = jnp.zeros_like(acc)

    row_i = lax.broadcasted_iota(jnp.int32, (LANES, orbs), 0)
    row_k = lax.broadcasted_iota(jnp.int32, (LANES, orbs), 1)
    down = jnp.where((row_i % orbs == row_k) & (row_i < used), 1.0, 0.0).astype(jnp.bfloat16)
    col_i = lax.broadcasted_iota(jnp.int32, (orbs, LANES), 1)
    col_k = lax.broadcasted_iota(jnp.int32, (orbs, LANES), 0)
    across = jnp.where((col_i % orbs == col_k) & (col_i < used), 1.0, 0.0).astype(jnp.bfloat16)
    on_diag = (
        lax.broadcasted_iota(jnp.int32, (LANES, LANES), 0) // orbs
        == lax.broadcasted_iota(jnp.int32, (LANES, LANES), 1) // orbs
    )
    diag_mask = jnp.where(on_diag, 1.0, 0.0)

    @pl.loop(0, modes)
    def _(m):
        spread = lax.dot_general(
            down, coup_ref[m], (((1,), (1,)), ((), ())), preferred_element_type=jnp.float32
        ).astype(jnp.bfloat16)
        full = jnp.dot(spread, across, preferred_element_type=jnp.float32)
        diag[m] = (full * diag_mask).astype(jnp.bfloat16)

    @pl.loop(0, modes // group)
    def _(g):
        @pl.loop(0, group)
        def _(n):
            m = g * group + n
            low = occ_ref[m]
            high = low + 1.0
            up = shift_ref[m] + pad
            dn = pad - shift_ref[m]
            up_t, up_r = lax.div(up, per), lax.rem(up, per)
            dn_t, dn_r = lax.div(dn, per), lax.rem(dn, per)
            upper = copies[up_r, pl.ds(up_t, tiles)]
            lower = copies[dn_r, pl.ds(dn_t, tiles)]
            shifted = (high * upper + low * lower).reshape(tiles * rows, LANES)
            right = jnp.dot(
                shifted.astype(jnp.bfloat16), diag[m], preferred_element_type=jnp.float32
            )
            at = pl.multiple_of(n * slot, 16)
            rights[:, pl.ds(at, rows), :] = right.reshape(tiles, rows, LANES).astype(jnp.bfloat16)

        left = pair_ref[g]

        @pl.loop(0, tiles)
        def _(t):
            acc[t] += jnp.dot(left, rights[t], preferred_element_type=jnp.float32)

    out_ref[...] = acc[...].astype(out_ref.dtype)


def correlate(green, mats_flat, occ, shifts, out_type):
    count_e, flat = green.shape
    orbs = math.isqrt(flat // 2)
    modes = mats_flat.shape[0]
    span = count_e // 2
    per = LANES // orbs
    rows = 2 * orbs
    slot = ceil_div(rows, 16) * 16
    tiles = ceil_div(count_e, per)
    pad_tiles = ceil_div(span, per)
    stored = tiles + 2 * pad_tiles
    group = math.gcd(16 if tiles <= 24 else 8, modes)

    blocks = jnp.pad(green.reshape(count_e, rows, orbs), ((0, tiles * per - count_e), (0, 0), (0, 0)))
    blocks = blocks.reshape(tiles, per, rows, orbs).transpose(0, 2, 1, 3)
    blocks = blocks.reshape(tiles, rows, per * orbs)
    blocks = jnp.pad(blocks, ((1, 1), (0, 0), (0, LANES - per * orbs)))
    mats = mats_flat.reshape(modes, orbs, orbs)
    sides = mats.reshape(modes // group, group, orbs, orbs).transpose(0, 2, 1, 3)
    zero = jnp.zeros_like(sides)
    pair = jnp.stack(
        [jnp.concatenate([sides, zero], -1), jnp.concatenate([zero, sides], -1)], 1
    ).reshape(modes // group, rows, group, rows)
    pair = jnp.pad(pair, ((0, 0), (0, 0), (0, 0), (0, slot - rows)))
    pair = pair.reshape(modes // group, rows, group * slot)

    sizes = (orbs, per, tiles, pad_tiles, stored, group, rows, slot)
    vmem = pl.BlockSpec(memory_space=pltpu.VMEM)
    smem = pl.BlockSpec(memory_space=pltpu.SMEM)
    out = pl.pallas_call(
        functools.partial(kernel, sizes),
        out_shape=jax.ShapeDtypeStruct((tiles, rows, LANES), out_type),
        in_specs=[smem, smem, vmem, vmem, vmem],
        out_specs=vmem,
        scratch_shapes=[
            pltpu.VMEM((per, stored, rows, LANES), jnp.float32),
            pltpu.VMEM((modes, LANES, LANES), jnp.bfloat16),
            pltpu.VMEM((tiles, group * slot, LANES), jnp.bfloat16),
            pltpu.VMEM((tiles, rows, LANES), jnp.float32),
        ],
        compiler_params=pltpu.CompilerParams(vmem_limit_bytes=62 * 1024 * 1024),
        cost_estimate=pl.CostEstimate(
            flops=modes * count_e * flat * orbs * 4, bytes_accessed=4 * count_e * flat, transcendentals=0
        ),
    )(occ, shifts, blocks, mats, pair)
    out = out[:, :, : per * orbs].reshape(tiles, rows, per, orbs).transpose(0, 2, 1, 3)
    return out.reshape(tiles * per, flat)[:count_e]


def on_device(green_less, coupling, occupation, shift_index):
    n_slab = lax.axis_size("slab")
    local_slabs = green_less.shape[0]
    count_b = coupling.shape[1]

    def elements(green, mats, occ, shifts, out_type):
        return jnp.stack(
            [correlate(green[:, b], mats[b], occ, shifts, out_type) for b in range(count_b)], 1
        )

    if n_slab == 1:
        results = []
        owned = [
            lax.all_to_all(green_less[s], "energy", split_axis=1, concat_axis=0, tiled=True)
            for s in range(local_slabs)
        ]
        for s in range(local_slabs):
            sigma = elements(owned[s], coupling[s], occupation, shift_index, jnp.bfloat16)
            results.append(
                lax.all_to_all(sigma, "energy", split_axis=0, concat_axis=1, tiled=True)
            )
        return jnp.stack(results)
    owned = lax.all_to_all(green_less, "energy", split_axis=2, concat_axis=1, tiled=True)
    side = lax.axis_index("slab")
    half = coupling.shape[2]
    first = side * half
    occ_half = lax.dynamic_slice_in_dim(occupation, first, half)
    shift_half = lax.dynamic_slice_in_dim(shift_index, first, half)
    own_mats = lax.dynamic_index_in_dim(coupling, side, 0, keepdims=False)
    other_mats = lax.dynamic_index_in_dim(coupling, 1 - side, 0, keepdims=False)
    partner = partner_2(owned[0], "slab", 0)
    mine = elements(owned[0], own_mats, occ_half, shift_half, jnp.float32)
    theirs = elements(partner, other_mats, occ_half, shift_half, jnp.float32)
    total = (mine + partner_2(theirs, "slab", 0))[None]
    sigma = total.astype(jnp.bfloat16)
    return lax.all_to_all(sigma, "energy", split_axis=1, concat_axis=2, tiled=True)


def solution(mesh):
    return jax.shard_map(
        on_device,
        mesh=mesh,
        in_specs=(P("slab", "energy", None, None), P(None, "energy", "slab", None), P(), P()),
        out_specs=P("slab", "energy", None, None),
        check_vma=False,
    )
```

```python
import functools
import math

import jax
import jax.numpy as jnp
from jax import lax
from jax.experimental import pallas as pl
from jax.experimental.pallas import tpu as pltpu
from jax.sharding import PartitionSpec as P

LANES = 256


def partner_2(value, axis, distance):
    mask = 2**distance
    pairs = [(source, source ^ mask) for source in range(lax.axis_size(axis))]
    return lax.ppermute(value, axis, pairs)


def ceil_div(a, b):
    return (a + b - 1) // b


def spread_kernel(orbs, per, mats_ref, out_ref, wide):
    used = per * orbs
    modes, depth, _ = mats_ref.shape
    col_i = lax.broadcasted_iota(jnp.int32, (orbs, LANES), 1)
    col_k = lax.broadcasted_iota(jnp.int32, (orbs, LANES), 0)
    across = jnp.where((col_i % orbs == col_k) & (col_i < used), 1.0, 0.0).astype(jnp.bfloat16)
    wide[...] = (
        jnp.dot(
            mats_ref[...].reshape(modes * depth, orbs), across, preferred_element_type=jnp.float32
        )
        .astype(jnp.bfloat16)
        .reshape(modes, depth, LANES)
    )
    row_i = lax.broadcasted_iota(jnp.int32, (LANES, depth), 0)
    row_k = lax.broadcasted_iota(jnp.int32, (LANES, depth), 1)
    down = jnp.where((row_i % orbs == row_k) & (row_i < used), 1.0, 0.0).astype(jnp.bfloat16)
    on_diag = (
        lax.broadcasted_iota(jnp.int32, (LANES, LANES), 0) // orbs
        == lax.broadcasted_iota(jnp.int32, (LANES, LANES), 1) // orbs
    )
    mask = jnp.where(on_diag, 1.0, 0.0)
    for m in range(modes):
        full = jnp.dot(down, wide[m], preferred_element_type=jnp.float32)
        out_ref[m] = (full * mask).astype(jnp.bfloat16)


def kernel(
    sizes, occ_ref, shift_ref, green_ref, diag_ref, pair_ref, out_ref, copies, rights, acc
):
    orbs, per, tiles, pad_tiles, stored, group, rows, slot = sizes
    used = per * orbs
    pad = pad_tiles * per
    g = pl.program_id(0)

    @pl.when(g == 0)
    def _():
        edge = pad_tiles - 1
        copies[:, :edge] = jnp.zeros((per, edge, rows, LANES), jnp.float32)
        tail = stored - (pad_tiles + tiles)
        copies[:, pad_tiles + tiles :] = jnp.zeros((per, tail, rows, LANES), jnp.float32)
        lane = lax.broadcasted_iota(jnp.int32, (rows, LANES), 1)

        @pl.loop(0, tiles + 1)
        def _(t):
            here = green_ref[t].astype(jnp.float32)
            after = green_ref[t + 1].astype(jnp.float32)
            at = edge + t
            copies[0, at] = here
            for r in range(1, per):
                cut = used - orbs * r
                copies[r, at] = jnp.where(
                    lane < cut,
                    pltpu.roll(here, LANES - orbs * r, 1),
                    pltpu.roll(after, cut, 1),
                )

        if slot > rows:
            for n in range(group):
                low_edge = rows // 16 * 16
                rights[:, n * slot + low_edge : (n + 1) * slot, :] = jnp.zeros(
                    (tiles, slot - low_edge, LANES), jnp.bfloat16
                )
        acc[...] = jnp.zeros_like(acc)

    @pl.loop(0, group, unroll=4)
    def _(n):
        m = g * group + n
        low = occ_ref[m]
        high = low + 1.0
        up = shift_ref[m] + pad
        dn = pad - shift_ref[m]
        up_t, up_r = lax.div(up, per), lax.rem(up, per)
        dn_t, dn_r = lax.div(dn, per), lax.rem(dn, per)
        upper = copies[up_r, pl.ds(up_t, tiles)]
        lower = copies[dn_r, pl.ds(dn_t, tiles)]
        shifted = (high * upper + low * lower).reshape(tiles * rows, LANES)
        right = jnp.dot(
            shifted.astype(jnp.bfloat16), diag_ref[n], preferred_element_type=jnp.float32
        )
        at = pl.multiple_of(n * slot, 16)
        rights[:, pl.ds(at, rows), :] = right.reshape(tiles, rows, LANES).astype(jnp.bfloat16)

    left = pair_ref[0]
    for t in range(tiles):
        acc[t] += jnp.dot(left, rights[t], preferred_element_type=jnp.float32)

    @pl.when(g == pl.num_programs(0) - 1)
    def _():
        out_ref[...] = acc[...].astype(out_ref.dtype)


def spread_mats(mats_flat):
    modes, flat = mats_flat.shape
    orbs = math.isqrt(flat)
    depth = ceil_div(orbs, 16) * 16
    group = math.gcd(16, modes)
    turned = mats_flat.reshape(modes, orbs, orbs).transpose(0, 2, 1)
    turned = jnp.pad(turned, ((0, 0), (0, depth - orbs), (0, 0)))
    return pl.pallas_call(
        functools.partial(spread_kernel, orbs, LANES // orbs),
        grid=(modes // group,),
        out_shape=jax.ShapeDtypeStruct((modes, LANES, LANES), jnp.bfloat16),
        in_specs=[pl.BlockSpec((group, depth, orbs), lambda g: (g, 0, 0))],
        out_specs=pl.BlockSpec((group, LANES, LANES), lambda g: (g, 0, 0)),
        scratch_shapes=[pltpu.VMEM((group, depth, LANES), jnp.bfloat16)],
        compiler_params=pltpu.CompilerParams(vmem_limit_bytes=24 * 1024 * 1024),
        cost_estimate=pl.CostEstimate(
            flops=modes * LANES * LANES * LANES * 2,
            bytes_accessed=2 * modes * LANES * LANES,
            transcendentals=0,
        ),
    )(turned)


def mode_group(count_e, modes):
    return math.gcd(16 if count_e <= 160 else 8, modes)


def pair_mats(mats_flat, group):
    modes, flat = mats_flat.shape
    orbs = math.isqrt(flat)
    rows = 2 * orbs
    slot = ceil_div(rows, 16) * 16
    sides = mats_flat.reshape(modes // group, group, orbs, orbs).transpose(0, 2, 1, 3)
    zero = jnp.zeros_like(sides)
    pair = jnp.stack(
        [jnp.concatenate([sides, zero], -1), jnp.concatenate([zero, sides], -1)], 1
    ).reshape(modes // group, rows, group, rows)
    pair = jnp.pad(pair, ((0, 0), (0, 0), (0, 0), (0, slot - rows)))
    return pair.reshape(modes // group, rows, group * slot)


def correlate(green, mats_flat, occ, shifts, out_type):
    count_e, flat = green.shape
    orbs = math.isqrt(flat // 2)
    modes = mats_flat.shape[0]
    span = count_e // 2
    per = LANES // orbs
    rows = 2 * orbs
    slot = ceil_div(rows, 16) * 16
    tiles = ceil_div(count_e, per)
    pad_tiles = ceil_div(span, per)
    stored = tiles + 2 * pad_tiles
    group = mode_group(count_e, modes)
    diag = spread_mats(mats_flat)
    pair = pair_mats(mats_flat, group)

    blocks = jnp.pad(green.reshape(count_e, rows, orbs), ((0, tiles * per - count_e), (0, 0), (0, 0)))
    blocks = blocks.reshape(tiles, per, rows, orbs).transpose(0, 2, 1, 3)
    blocks = blocks.reshape(tiles, rows, per * orbs)
    blocks = jnp.pad(blocks, ((1, 1), (0, 0), (0, LANES - per * orbs)))

    sizes = (orbs, per, tiles, pad_tiles, stored, group, rows, slot)
    smem = pl.BlockSpec(memory_space=pltpu.SMEM)
    whole = lambda shape: pl.BlockSpec(shape, lambda g: (0,) * len(shape))
    out = pl.pallas_call(
        functools.partial(kernel, sizes),
        grid=(modes // group,),
        out_shape=jax.ShapeDtypeStruct((tiles, rows, LANES), out_type),
        in_specs=[
            smem,
            smem,
            whole((tiles + 2, rows, LANES)),
            pl.BlockSpec((group, LANES, LANES), lambda g: (g, 0, 0)),
            pl.BlockSpec((1, rows, group * slot), lambda g: (g, 0, 0)),
        ],
        out_specs=whole((tiles, rows, LANES)),
        scratch_shapes=[
            pltpu.VMEM((per, stored, rows, LANES), jnp.float32),
            pltpu.VMEM((tiles, group * slot, LANES), jnp.bfloat16),
            pltpu.VMEM((tiles, rows, LANES), jnp.float32),
        ],
        compiler_params=pltpu.CompilerParams(vmem_limit_bytes=62 * 1024 * 1024),
        cost_estimate=pl.CostEstimate(
            flops=modes * count_e * flat * orbs * 4,
            bytes_accessed=2 * modes * LANES * LANES,
            transcendentals=0,
        ),
    )(occ, shifts, blocks, diag, pair)
    out = out[:, :, : per * orbs].reshape(tiles, rows, per, orbs).transpose(0, 2, 1, 3)
    return out.reshape(tiles * per, flat)[:count_e]


def on_device(green_less, coupling, occupation, shift_index):
    n_slab = lax.axis_size("slab")
    local_slabs = green_less.shape[0]
    count_b = coupling.shape[1]

    def elements(green, mats, occ, shifts, out_type):
        return jnp.stack(
            [correlate(green[:, b], mats[b], occ, shifts, out_type) for b in range(count_b)], 1
        )

    if n_slab == 1:
        results = []
        owned = [
            lax.all_to_all(green_less[s], "energy", split_axis=1, concat_axis=0, tiled=True)
            for s in range(local_slabs)
        ]
        for s in range(local_slabs):
            sigma = elements(owned[s], coupling[s], occupation, shift_index, jnp.bfloat16)
            results.append(
                lax.all_to_all(sigma, "energy", split_axis=0, concat_axis=1, tiled=True)
            )
        return jnp.stack(results)
    owned = lax.all_to_all(green_less, "energy", split_axis=2, concat_axis=1, tiled=True)
    side = lax.axis_index("slab")
    half = coupling.shape[2]
    first = side * half
    occ_half = lax.dynamic_slice_in_dim(occupation, first, half)
    shift_half = lax.dynamic_slice_in_dim(shift_index, first, half)
    own_mats = lax.dynamic_index_in_dim(coupling, side, 0, keepdims=False)
    other_mats = lax.dynamic_index_in_dim(coupling, 1 - side, 0, keepdims=False)
    partner = partner_2(owned[0], "slab", 0)
    mine = elements(owned[0], own_mats, occ_half, shift_half, jnp.float32)
    theirs = elements(partner, other_mats, occ_half, shift_half, jnp.float32)
    total = (mine + partner_2(theirs, "slab", 0))[None]
    sigma = total.astype(jnp.bfloat16)
    return lax.all_to_all(sigma, "energy", split_axis=1, concat_axis=2, tiled=True)


def solution(mesh):
    return jax.shard_map(
        on_device,
        mesh=mesh,
        in_specs=(P("slab", "energy", None, None), P(None, "energy", "slab", None), P(), P()),
        out_specs=P("slab", "energy", None, None),
        check_vma=False,
    )
```

```python
import functools
import math

import jax
import jax.numpy as jnp
from jax import lax
from jax.experimental import pallas as pl
from jax.experimental.pallas import tpu as pltpu
from jax.sharding import PartitionSpec as P

LANES = 256


def partner_2(value, axis, distance):
    mask = 2**distance
    pairs = [(source, source ^ mask) for source in range(lax.axis_size(axis))]
    return lax.ppermute(value, axis, pairs)


def ceil_div(a, b):
    return (a + b - 1) // b


def spread(orbs, per, mats_ref, out_ref, wide):
    used = per * orbs
    modes, depth, _ = mats_ref.shape
    col_i = lax.broadcasted_iota(jnp.int32, (orbs, LANES), 1)
    col_k = lax.broadcasted_iota(jnp.int32, (orbs, LANES), 0)
    across = jnp.where((col_i % orbs == col_k) & (col_i < used), 1.0, 0.0).astype(jnp.bfloat16)
    wide[...] = (
        jnp.dot(
            mats_ref[...].reshape(modes * depth, orbs), across, preferred_element_type=jnp.float32
        )
        .astype(jnp.bfloat16)
        .reshape(modes, depth, LANES)
    )
    row_i = lax.broadcasted_iota(jnp.int32, (LANES, depth), 0)
    row_k = lax.broadcasted_iota(jnp.int32, (LANES, depth), 1)
    down = jnp.where((row_i % orbs == row_k) & (row_i < used), 1.0, 0.0).astype(jnp.bfloat16)
    on_diag = (
        lax.broadcasted_iota(jnp.int32, (LANES, LANES), 0) // orbs
        == lax.broadcasted_iota(jnp.int32, (LANES, LANES), 1) // orbs
    )
    mask = jnp.where(on_diag, 1.0, 0.0)
    for m in range(modes):
        full = jnp.dot(down, wide[m], preferred_element_type=jnp.float32)
        out_ref[m] = (full * mask).astype(jnp.bfloat16)


def kernel(
    sizes, occ_ref, shift_ref, green_ref, mats_ref, pair_ref, out_ref, copies, rights, acc, diag, wide
):
    orbs, per, tiles, pad_tiles, stored, group, rows, slot = sizes
    used = per * orbs
    pad = pad_tiles * per
    g = pl.program_id(0)

    @pl.when(g == 0)
    def _():
        edge = pad_tiles - 1
        copies[:, :edge] = jnp.zeros((per, edge, rows, LANES), jnp.float32)
        tail = stored - (pad_tiles + tiles)
        copies[:, pad_tiles + tiles :] = jnp.zeros((per, tail, rows, LANES), jnp.float32)
        lane = lax.broadcasted_iota(jnp.int32, (rows, LANES), 1)

        @pl.loop(0, tiles + 1)
        def _(t):
            here = green_ref[t].astype(jnp.float32)
            after = green_ref[t + 1].astype(jnp.float32)
            at = edge + t
            copies[0, at] = here
            for r in range(1, per):
                cut = used - orbs * r
                copies[r, at] = jnp.where(
                    lane < cut,
                    pltpu.roll(here, LANES - orbs * r, 1),
                    pltpu.roll(after, cut, 1),
                )

        if slot > rows:
            for n in range(group):
                low_edge = rows // 16 * 16
                rights[:, n * slot + low_edge : (n + 1) * slot, :] = jnp.zeros(
                    (tiles, slot - low_edge, LANES), jnp.bfloat16
                )
        acc[...] = jnp.zeros_like(acc)

    spread(orbs, per, mats_ref, diag, wide)

    @pl.loop(0, group, unroll=4)
    def _(n):
        m = g * group + n
        low = occ_ref[m]
        high = low + 1.0
        up = shift_ref[m] + pad
        dn = pad - shift_ref[m]
        up_t, up_r = lax.div(up, per), lax.rem(up, per)
        dn_t, dn_r = lax.div(dn, per), lax.rem(dn, per)
        upper = copies[up_r, pl.ds(up_t, tiles)]
        lower = copies[dn_r, pl.ds(dn_t, tiles)]
        shifted = (high * upper + low * lower).reshape(tiles * rows, LANES)
        right = jnp.dot(
            shifted.astype(jnp.bfloat16), diag[n], preferred_element_type=jnp.float32
        )
        at = pl.multiple_of(n * slot, 16)
        rights[:, pl.ds(at, rows), :] = right.reshape(tiles, rows, LANES).astype(jnp.bfloat16)

    left = pair_ref[0]
    for t in range(tiles):
        acc[t] += jnp.dot(left, rights[t], preferred_element_type=jnp.float32)

    @pl.when(g == pl.num_programs(0) - 1)
    def _():
        out_ref[...] = acc[...].astype(out_ref.dtype)


def turn_mats(mats_flat):
    modes, flat = mats_flat.shape
    orbs = math.isqrt(flat)
    depth = ceil_div(orbs, 16) * 16
    turned = mats_flat.reshape(modes, orbs, orbs).transpose(0, 2, 1)
    return jnp.pad(turned, ((0, 0), (0, depth - orbs), (0, 0)))


def mode_group(count_e, modes):
    return math.gcd(16 if count_e <= 160 else 8, modes)


def pair_mats(mats_flat, group):
    modes, flat = mats_flat.shape
    orbs = math.isqrt(flat)
    rows = 2 * orbs
    slot = ceil_div(rows, 16) * 16
    sides = mats_flat.reshape(modes // group, group, orbs, orbs).transpose(0, 2, 1, 3)
    zero = jnp.zeros_like(sides)
    pair = jnp.stack(
        [jnp.concatenate([sides, zero], -1), jnp.concatenate([zero, sides], -1)], 1
    ).reshape(modes // group, rows, group, rows)
    pair = jnp.pad(pair, ((0, 0), (0, 0), (0, 0), (0, slot - rows)))
    return pair.reshape(modes // group, rows, group * slot)


def correlate(green, mats_flat, occ, shifts, out_type):
    count_e, flat = green.shape
    orbs = math.isqrt(flat // 2)
    modes = mats_flat.shape[0]
    span = count_e // 2
    per = LANES // orbs
    rows = 2 * orbs
    slot = ceil_div(rows, 16) * 16
    tiles = ceil_div(count_e, per)
    pad_tiles = ceil_div(span, per)
    stored = tiles + 2 * pad_tiles
    group = mode_group(count_e, modes)
    turned = turn_mats(mats_flat)
    depth = turned.shape[1]
    pair = pair_mats(mats_flat, group)

    blocks = jnp.pad(green.reshape(count_e, rows, orbs), ((0, tiles * per - count_e), (0, 0), (0, 0)))
    blocks = blocks.reshape(tiles, per, rows, orbs).transpose(0, 2, 1, 3)
    blocks = blocks.reshape(tiles, rows, per * orbs)
    blocks = jnp.pad(blocks, ((1, 1), (0, 0), (0, LANES - per * orbs)))

    sizes = (orbs, per, tiles, pad_tiles, stored, group, rows, slot)
    smem = pl.BlockSpec(memory_space=pltpu.SMEM)
    whole = lambda shape: pl.BlockSpec(shape, lambda g: (0,) * len(shape))
    out = pl.pallas_call(
        functools.partial(kernel, sizes),
        grid=(modes // group,),
        out_shape=jax.ShapeDtypeStruct((tiles, rows, LANES), out_type),
        in_specs=[
            smem,
            smem,
            whole((tiles + 2, rows, LANES)),
            pl.BlockSpec((group, depth, orbs), lambda g: (g, 0, 0)),
            pl.BlockSpec((1, rows, group * slot), lambda g: (g, 0, 0)),
        ],
        out_specs=whole((tiles, rows, LANES)),
        scratch_shapes=[
            pltpu.VMEM((per, stored, rows, LANES), jnp.float32),
            pltpu.VMEM((tiles, group * slot, LANES), jnp.bfloat16),
            pltpu.VMEM((tiles, rows, LANES), jnp.float32),
            pltpu.VMEM((group, LANES, LANES), jnp.bfloat16),
            pltpu.VMEM((group, depth, LANES), jnp.bfloat16),
        ],
        compiler_params=pltpu.CompilerParams(vmem_limit_bytes=62 * 1024 * 1024),
        cost_estimate=pl.CostEstimate(
            flops=modes * count_e * flat * orbs * 4,
            bytes_accessed=2 * modes * LANES * LANES,
            transcendentals=0,
        ),
    )(occ, shifts, blocks, turned, pair)
    out = out[:, :, : per * orbs].reshape(tiles, rows, per, orbs).transpose(0, 2, 1, 3)
    return out.reshape(tiles * per, flat)[:count_e]


def on_device(green_less, coupling, occupation, shift_index):
    n_slab = lax.axis_size("slab")
    local_slabs = green_less.shape[0]
    count_b = coupling.shape[1]

    def elements(green, mats, occ, shifts, out_type):
        return jnp.stack(
            [correlate(green[:, b], mats[b], occ, shifts, out_type) for b in range(count_b)], 1
        )

    if n_slab == 1:
        results = []
        owned = [
            lax.all_to_all(green_less[s], "energy", split_axis=1, concat_axis=0, tiled=True)
            for s in range(local_slabs)
        ]
        for s in range(local_slabs):
            sigma = elements(owned[s], coupling[s], occupation, shift_index, jnp.bfloat16)
            results.append(
                lax.all_to_all(sigma, "energy", split_axis=0, concat_axis=1, tiled=True)
            )
        return jnp.stack(results)
    owned = lax.all_to_all(green_less, "energy", split_axis=2, concat_axis=1, tiled=True)
    side = lax.axis_index("slab")
    half = coupling.shape[2]
    first = side * half
    occ_half = lax.dynamic_slice_in_dim(occupation, first, half)
    shift_half = lax.dynamic_slice_in_dim(shift_index, first, half)
    own_mats = lax.dynamic_index_in_dim(coupling, side, 0, keepdims=False)
    other_mats = lax.dynamic_index_in_dim(coupling, 1 - side, 0, keepdims=False)
    partner = partner_2(owned[0], "slab", 0)
    mine = elements(owned[0], own_mats, occ_half, shift_half, jnp.float32)
    theirs = elements(partner, other_mats, occ_half, shift_half, jnp.float32)
    total = (mine + partner_2(theirs, "slab", 0))[None]
    sigma = total.astype(jnp.bfloat16)
    return lax.all_to_all(sigma, "energy", split_axis=1, concat_axis=2, tiled=True)


def solution(mesh):
    return jax.shard_map(
        on_device,
        mesh=mesh,
        in_specs=(P("slab", "energy", None, None), P(None, "energy", "slab", None), P(), P()),
        out_specs=P("slab", "energy", None, None),
        check_vma=False,
    )
```

```python
import functools
import math

import jax
import jax.numpy as jnp
from jax import lax
from jax.experimental import pallas as pl
from jax.experimental.pallas import tpu as pltpu
from jax.sharding import PartitionSpec as P

LANES = 256


def partner_2(value, axis, distance):
    mask = 2**distance
    pairs = [(source, source ^ mask) for source in range(lax.axis_size(axis))]
    return lax.ppermute(value, axis, pairs)


def ceil_div(a, b):
    return (a + b - 1) // b


def spread(orbs, per, mats_ref, out_ref, wide):
    used = per * orbs
    modes, depth, _ = mats_ref.shape
    col_i = lax.broadcasted_iota(jnp.int32, (orbs, LANES), 1)
    col_k = lax.broadcasted_iota(jnp.int32, (orbs, LANES), 0)
    across = jnp.where((col_i % orbs == col_k) & (col_i < used), 1.0, 0.0).astype(jnp.bfloat16)
    wide[...] = (
        jnp.dot(
            mats_ref[...].reshape(modes * depth, orbs), across, preferred_element_type=jnp.float32
        )
        .astype(jnp.bfloat16)
        .reshape(modes, depth, LANES)
    )
    row_i = lax.broadcasted_iota(jnp.int32, (LANES, depth), 0)
    row_k = lax.broadcasted_iota(jnp.int32, (LANES, depth), 1)
    down = jnp.where((row_i % orbs == row_k) & (row_i < used), 1.0, 0.0).astype(jnp.bfloat16)
    on_diag = (
        lax.broadcasted_iota(jnp.int32, (LANES, LANES), 0) // orbs
        == lax.broadcasted_iota(jnp.int32, (LANES, LANES), 1) // orbs
    )
    mask = jnp.where(on_diag, 1.0, 0.0)
    for m in range(modes):
        full = jnp.dot(down, wide[m], preferred_element_type=jnp.float32)
        out_ref[m] = (full * mask).astype(jnp.bfloat16)


def kernel(
    sizes, occ_ref, shift_ref, green_ref, mats_ref, pair_ref, out_ref, copies, rights, acc, diag, wide
):
    orbs, per, tiles, pad_tiles, stored, group, rows, slot = sizes
    used = per * orbs
    pad = pad_tiles * per
    g = pl.program_id(0)

    @pl.when(g == 0)
    def _():
        edge = pad_tiles - 1
        copies[:, :edge] = jnp.zeros((per, edge, rows, LANES), jnp.float32)
        tail = stored - (pad_tiles + tiles)
        copies[:, pad_tiles + tiles :] = jnp.zeros((per, tail, rows, LANES), jnp.float32)
        lane = lax.broadcasted_iota(jnp.int32, (rows, LANES), 1)

        @pl.loop(0, tiles + 1)
        def _(t):
            here = green_ref[t].astype(jnp.float32)
            after = green_ref[t + 1].astype(jnp.float32)
            at = edge + t
            copies[0, at] = here
            for r in range(1, per):
                cut = used - orbs * r
                copies[r, at] = jnp.where(
                    lane < cut,
                    pltpu.roll(here, LANES - orbs * r, 1),
                    pltpu.roll(after, cut, 1),
                )

        if slot > rows:
            for n in range(group):
                low_edge = rows // 16 * 16
                rights[:, n * slot + low_edge : (n + 1) * slot, :] = jnp.zeros(
                    (tiles, slot - low_edge, LANES), jnp.bfloat16
                )
        acc[...] = jnp.zeros_like(acc)

    spread(orbs, per, mats_ref, diag, wide)

    @pl.loop(0, group, unroll=8)
    def _(n):
        m = g * group + n
        low = occ_ref[m]
        high = low + 1.0
        up = shift_ref[m] + pad
        dn = pad - shift_ref[m]
        up_t, up_r = lax.div(up, per), lax.rem(up, per)
        dn_t, dn_r = lax.div(dn, per), lax.rem(dn, per)
        upper = copies[up_r, pl.ds(up_t, tiles)]
        lower = copies[dn_r, pl.ds(dn_t, tiles)]
        shifted = (high * upper + low * lower).reshape(tiles * rows, LANES)
        right = jnp.dot(
            shifted.astype(jnp.bfloat16), diag[n], preferred_element_type=jnp.float32
        )
        at = pl.multiple_of(n * slot, 16)
        rights[:, pl.ds(at, rows), :] = right.reshape(tiles, rows, LANES).astype(jnp.bfloat16)

    left = pair_ref[0]
    for t in range(tiles):
        acc[t] += jnp.dot(left, rights[t], preferred_element_type=jnp.float32)

    @pl.when(g == pl.num_programs(0) - 1)
    def _():
        out_ref[...] = acc[...].astype(out_ref.dtype)


def turn_mats(mats_flat):
    modes, flat = mats_flat.shape
    orbs = math.isqrt(flat)
    depth = ceil_div(orbs, 16) * 16
    turned = mats_flat.reshape(modes, orbs, orbs).transpose(0, 2, 1)
    return jnp.pad(turned, ((0, 0), (0, depth - orbs), (0, 0)))


def mode_group(count_e, modes):
    return math.gcd(16 if count_e <= 160 else 8, modes)


def pair_mats(mats_flat, group):
    modes, flat = mats_flat.shape
    orbs = math.isqrt(flat)
    rows = 2 * orbs
    slot = ceil_div(rows, 16) * 16
    sides = mats_flat.reshape(modes // group, group, orbs, orbs).transpose(0, 2, 1, 3)
    zero = jnp.zeros_like(sides)
    pair = jnp.stack(
        [jnp.concatenate([sides, zero], -1), jnp.concatenate([zero, sides], -1)], 1
    ).reshape(modes // group, rows, group, rows)
    pair = jnp.pad(pair, ((0, 0), (0, 0), (0, 0), (0, slot - rows)))
    return pair.reshape(modes // group, rows, group * slot)


def correlate(green, mats_flat, occ, shifts, out_type):
    count_e, flat = green.shape
    orbs = math.isqrt(flat // 2)
    modes = mats_flat.shape[0]
    span = count_e // 2
    per = LANES // orbs
    rows = 2 * orbs
    slot = ceil_div(rows, 16) * 16
    tiles = ceil_div(count_e, per)
    pad_tiles = ceil_div(span, per)
    stored = tiles + 2 * pad_tiles
    group = mode_group(count_e, modes)
    turned = turn_mats(mats_flat)
    depth = turned.shape[1]
    pair = pair_mats(mats_flat, group)

    after = (tiles + 1) * per - count_e
    blocks = jnp.pad(green, ((per, after), (0, 0))).reshape(tiles + 2, per, rows, orbs)
    blocks = blocks.transpose(0, 2, 1, 3).reshape(tiles + 2, rows, per * orbs)
    blocks = jnp.pad(blocks, ((0, 0), (0, 0), (0, LANES - per * orbs)))

    sizes = (orbs, per, tiles, pad_tiles, stored, group, rows, slot)
    smem = pl.BlockSpec(memory_space=pltpu.SMEM)
    whole = lambda shape: pl.BlockSpec(shape, lambda g: (0,) * len(shape))
    out = pl.pallas_call(
        functools.partial(kernel, sizes),
        grid=(modes // group,),
        out_shape=jax.ShapeDtypeStruct((tiles, rows, LANES), out_type),
        in_specs=[
            smem,
            smem,
            whole((tiles + 2, rows, LANES)),
            pl.BlockSpec((group, depth, orbs), lambda g: (g, 0, 0)),
            pl.BlockSpec((1, rows, group * slot), lambda g: (g, 0, 0)),
        ],
        out_specs=whole((tiles, rows, LANES)),
        scratch_shapes=[
            pltpu.VMEM((per, stored, rows, LANES), jnp.float32),
            pltpu.VMEM((tiles, group * slot, LANES), jnp.bfloat16),
            pltpu.VMEM((tiles, rows, LANES), jnp.float32),
            pltpu.VMEM((group, LANES, LANES), jnp.bfloat16),
            pltpu.VMEM((group, depth, LANES), jnp.bfloat16),
        ],
        compiler_params=pltpu.CompilerParams(vmem_limit_bytes=62 * 1024 * 1024),
        cost_estimate=pl.CostEstimate(
            flops=modes * count_e * flat * orbs * 4,
            bytes_accessed=2 * modes * LANES * LANES,
            transcendentals=0,
        ),
    )(occ, shifts, blocks, turned, pair)
    out = out[:, :, : per * orbs].reshape(tiles, rows, per, orbs).transpose(0, 2, 1, 3)
    return out.reshape(tiles * per, flat)[:count_e]


def on_device(green_less, coupling, occupation, shift_index):
    n_slab = lax.axis_size("slab")
    local_slabs = green_less.shape[0]
    count_b = coupling.shape[1]

    def elements(green, mats, occ, shifts, out_type):
        return jnp.stack(
            [correlate(green[:, b], mats[b], occ, shifts, out_type) for b in range(count_b)], 1
        )

    if n_slab == 1:
        results = []
        owned = [
            lax.all_to_all(green_less[s], "energy", split_axis=1, concat_axis=0, tiled=True)
            for s in range(local_slabs)
        ]
        for s in range(local_slabs):
            sigma = elements(owned[s], coupling[s], occupation, shift_index, jnp.bfloat16)
            count = lax.axis_size("energy")
            parts = sigma.reshape(count, sigma.shape[0] // count, count_b, sigma.shape[-1])
            parts = lax.all_to_all(parts, "energy", split_axis=0, concat_axis=0, tiled=True)
            parts = parts.transpose(1, 0, 2, 3)
            results.append(parts.reshape(parts.shape[0], count * count_b, parts.shape[-1]))
        return jnp.stack(results)
    owned = lax.all_to_all(green_less, "energy", split_axis=2, concat_axis=1, tiled=True)
    side = lax.axis_index("slab")
    half = coupling.shape[2]
    first = side * half
    occ_half = lax.dynamic_slice_in_dim(occupation, first, half)
    shift_half = lax.dynamic_slice_in_dim(shift_index, first, half)
    own_mats = lax.dynamic_index_in_dim(coupling, side, 0, keepdims=False)
    other_mats = lax.dynamic_index_in_dim(coupling, 1 - side, 0, keepdims=False)
    partner = partner_2(owned[0], "slab", 0)
    mine = elements(owned[0], own_mats, occ_half, shift_half, jnp.float32)
    theirs = elements(partner, other_mats, occ_half, shift_half, jnp.float32)
    total = (mine + partner_2(theirs, "slab", 0))[None]
    sigma = total.astype(jnp.bfloat16)
    return lax.all_to_all(sigma, "energy", split_axis=1, concat_axis=2, tiled=True)


def solution(mesh):
    return jax.shard_map(
        on_device,
        mesh=mesh,
        in_specs=(P("slab", "energy", None, None), P(None, "energy", "slab", None), P(), P()),
        out_specs=P("slab", "energy", None, None),
        check_vma=False,
    )
```
